256 devices in a mesh: dp: 4 (over x), seq: 64 (over y, z, core).
Axes of the slice: x: 4, y: 4, z: 8, core: 2. Of those that a mesh axis runs over, the one named last changes fastest.
Arguments:
- query: bfloat16 [4, 8192, 1024], P('dp', 'seq'), may hold values from -70 to 70
- keys: bfloat16 [4, 8192, 1024], P('dp', 'seq'), may hold values from -70 to 70
- values: bfloat16 [4, 8192, 1024], P('dp', 'seq'), may hold values from -6 to 6
- out_grad: bfloat16 [4, 8192, 2048], P('dp', 'seq'), may hold values from -16 to 16
- out_weight: bfloat16 [2048, 1024], P('seq'), may hold values from -0.125 to 0.125
- lengths: int32 [4, 32], P('dp'), may hold values from 128 to 512, as said below
Outputs:
- query_grad: bfloat16 [4, 8192, 1024], P('dp', 'seq')
- key_grad: bfloat16 [4, 8192, 1024], P('dp', 'seq')
- value_grad: bfloat16 [4, 8192, 1024], P('dp', 'seq')
- weight_grad: float32 [2048, 1024], P(('dp', 'seq'))
The draws below stay inside these ranges and needn't reach their ends.
Inputs may be any that keep to these rules, and one draw needn't show every extreme that they name: The lengths of a pack sum to 8192, each is a multiple of a quarter of 128, and in every pack one image has exactly 512 tokens.
All inputs are finite; a program needn't handle non-finite values.
Results may differ from the reference program's by a relative error of at most 0.04.
Values may be sent and summed in bfloat16 or wider, within the bound.
No kernel may reach another device: no remote copies, remote signals or barrier semaphores. Data moves between devices by JAX's collectives and lax.ppermute only.
A program may use at most 128 MiB of HBM per device.

```python
import math
import jax
import jax.numpy as jnp
from jax import lax

D = 2048
HEADS = 8
HEAD = 128
REACH = 4
TOK_DEV = 128
PACKS = 4
TOKENS = 8192
IMAGES = 32


def pair_fields(key, chosen_rate, strongest):
    field_shape = (PACKS, TOKENS, HEADS * HEAD)
    key_keys, key_query, key_chosen, key_strength = jax.random.split(key, 4)
    keys_field = jax.random.truncated_normal(key_keys, -4.0, 4.0, field_shape, jnp.float32)
    query_field = jax.random.truncated_normal(key_query, -4.0, 4.0, field_shape, jnp.float32)
    chosen = jax.random.bernoulli(key_chosen, chosen_rate, (PACKS, TOKENS, 1))
    strength = jax.random.uniform(key_strength, (PACKS, TOKENS, 1), jnp.float32, 0.3 * strongest, strongest)
    query_field = jnp.where(chosen, strength * keys_field, query_field)
    previous = jnp.roll(keys_field, 1, axis=1)
    previous_chosen = jnp.roll(chosen, 1, axis=1)
    keys_field = jnp.where(previous_chosen & jnp.logical_not(chosen), 0.985 * previous, keys_field)
    return (query_field, keys_field)


def draw_query(key, part):
    fields = pair_fields(key, 0.0, 12.0)
    return fields[0].astype(jnp.bfloat16)


def draw_keys(key, part):
    fields = pair_fields(key, 0.0, 12.0)
    return fields[1].astype(jnp.bfloat16)


def draw_lengths(key, part):
    key = jax.random.fold_in(key, 11)
    ceiling = 4 * (REACH - 1)
    quarter = TOK_DEV // 4
    rows = []
    for pack_index in range(PACKS):
        pack_key = jax.random.fold_in(key, pack_index)
        split_key, order_key = jax.random.split(pack_key)
        image_keys = jax.random.split(split_key, IMAGES - 1)
        remaining = jnp.arange(IMAGES - 2, -1, -1, dtype=jnp.int32)

        def pick(left_units, inputs):
            image_key, later = inputs
            lowest = jnp.maximum(0, left_units - ceiling * later)
            highest = jnp.minimum(ceiling, left_units)
            units = jax.random.randint(image_key, (), lowest, highest + 1, dtype=jnp.int32)
            return (left_units - units, units)
        start_units = jnp.asarray(4 * IMAGES - ceiling, jnp.int32)
        left_over, picked = lax.scan(pick, start_units, (image_keys, remaining))
        units_all = jnp.concatenate([jnp.full((1,), ceiling, jnp.int32), picked], 0)
        order = jax.random.permutation(order_key, IMAGES)
        units_all = units_all[order]
        rows.append(TOK_DEV + quarter * units_all)
    return jnp.stack(rows, 0).astype(jnp.int32)


def raised(values, rng, source, target, blocks, factor):
    owner, partner = [(jnp.arange(values.shape[axis_at]) // (values.shape[axis_at] // blocks)).reshape([-1 if axis == axis_at else 1 for axis in range(values.ndim)]) for axis_at in (source, target)]
    chosen = jax.random.permutation(rng, blocks)[partner]
    strong = (owner == chosen) | (owner == (partner + blocks // 2) % blocks)
    return jnp.where(strong, factor * values, values)


def block_levels(stream_key, dims, cuts, low, largest):
    def one(dim, shards_of):
        draws = jax.random.uniform(jax.random.fold_in(jax.random.fold_in(stream_key, 6), dim), (shards_of,), jnp.float32, low / len(cuts), largest / len(cuts))
        return jnp.repeat(jnp.exp(draws), dims[dim] // shards_of).reshape((-1,) + (1,) * (len(dims) - dim - 1))

    gain = one(*cuts[0])
    for cut in cuts[1:]:
        gain = gain * one(*cut)
    return gain


def noise(rng, dims, scale, bound, pieces=(), held_as=jnp.bfloat16):
    array = scale * jax.random.normal(rng, dims, jnp.float32)
    if pieces:
        array = array * block_levels(rng, dims, pieces, -0.22, 0.18)
    return jnp.clip(array, -bound, bound).astype(held_as)


def heavy_noise(stream_key, dims, deviation, most, cuts, heavy, kind=jnp.bfloat16):
    result = deviation * jax.random.normal(stream_key, dims, jnp.float32)
    if cuts:
        result = result * block_levels(stream_key, dims, cuts, -0.22, 0.18)
    return jnp.clip(raised(result, jax.random.fold_in(stream_key, 3), *heavy), -most, most).astype(kind)


def setup_inputs(seed: int = 0) -> dict:
    seeds = jax.random.split(jax.random.key(seed), 7)
    return {
        "query": draw_query(jax.random.fold_in(seeds[6], 71), 0),
        "keys": draw_keys(jax.random.fold_in(seeds[6], 71), 0),
        "values": noise(seeds[2], (PACKS, TOKENS, HEADS * HEAD), 1.0, 6.0, ((0, 4), (1, 64))),
        "out_grad": heavy_noise(seeds[3], (PACKS, TOKENS, D), 1.0, 16.0, ((0, 4), (1, 64)), (1, 2, 64, 4.0)),
        "out_weight": noise(seeds[4], (D, HEADS * HEAD), D ** -0.5, 0.125, ((0, 64),)),
        "lengths": draw_lengths(jax.random.fold_in(seeds[6], 71), 0),
    }


def segments(lengths_row, first_pos, row_total, pack_tokens):
    positions = first_pos + jnp.arange(row_total, dtype=jnp.int32)
    image_ends = jnp.cumsum(lengths_row).astype(jnp.int32)
    segment = lax.optimization_barrier(jnp.sum((positions[:, None] >= image_ends[None, :]).astype(jnp.int32), axis=1))
    inside = (positions >= 0) & (positions < pack_tokens)
    return jnp.where(inside, segment, -1).astype(jnp.int32)

def reference(query, keys, values, out_grad, out_weight, lengths):
    score_scale = 1.0 / math.sqrt(HEAD)
    feature_width = HEADS * HEAD
    block_count = TOKENS // TOK_DEV
    margin = REACH * TOK_DEV
    window = (2 * REACH + 1) * TOK_DEV
    weight_grad = jnp.zeros((D, feature_width), jnp.float32)
    query_grads, key_grads, value_grads = ([], [], [])
    for pack_index in range(PACKS):
        attended_grad = jnp.dot(out_grad[pack_index], out_weight, preferred_element_type=jnp.float32).astype(jnp.bfloat16)
        padding = jnp.zeros((margin, feature_width), jnp.bfloat16)
        keys_padded = jnp.concatenate([padding, keys[pack_index], padding], 0)
        values_padded = jnp.concatenate([padding, values[pack_index], padding], 0)
        segment_all = segments(lengths[pack_index], -margin, TOKENS + 2 * margin, TOKENS)
        query_pack = query[pack_index]

        def one_block(carry, block_index):
            key_acc, value_acc = carry
            first = block_index * TOK_DEV
            query_block = lax.dynamic_slice_in_dim(query_pack, first, TOK_DEV, 0).reshape(TOK_DEV, HEADS, HEAD).astype(jnp.float32)
            grad_block = lax.dynamic_slice_in_dim(attended_grad, first, TOK_DEV, 0).reshape(TOK_DEV, HEADS, HEAD).astype(jnp.float32)
            keys_win = lax.dynamic_slice_in_dim(keys_padded, first, window, 0).reshape(window, HEADS, HEAD).astype(jnp.float32)
            values_win = lax.dynamic_slice_in_dim(values_padded, first, window, 0).reshape(window, HEADS, HEAD).astype(jnp.float32)
            segment_query = lax.dynamic_slice_in_dim(segment_all, first + margin, TOK_DEV, 0)
            segment_keys = lax.dynamic_slice_in_dim(segment_all, first, window, 0)
            scores = jnp.einsum('qhe,khe->hqk', query_block, keys_win) * score_scale
            taken = (segment_query[:, None] == segment_keys[None, :])[None]
            scores = jnp.where(taken, scores, -1e+30)
            row_peak = lax.optimization_barrier(jnp.max(scores, axis=2, keepdims=True))
            log_norm = row_peak + jnp.log(lax.optimization_barrier(jnp.sum(jnp.exp(scores - row_peak), axis=2, keepdims=True)))
            probs = jnp.exp(scores - log_norm)
            probs_low = lax.optimization_barrier(probs.astype(jnp.bfloat16)).astype(jnp.float32)
            attended = jnp.einsum('hqk,khe->qhe', probs_low, values_win).astype(jnp.bfloat16)
            attended_wide = attended.astype(jnp.float32)
            row_delta = lax.optimization_barrier(jnp.sum(grad_block * attended_wide, axis=2)).T
            dprobs = jnp.einsum('qhe,khe->hqk', grad_block, values_win)
            dscores = lax.optimization_barrier((probs * (dprobs - row_delta[:, :, None])).astype(jnp.bfloat16)).astype(jnp.float32)
            query_part = (jnp.einsum('hqk,khe->qhe', dscores, keys_win) * score_scale).reshape(TOK_DEV, feature_width).astype(jnp.bfloat16)
            key_part = (jnp.einsum('hqk,qhe->khe', dscores, query_block) * score_scale).reshape(window, feature_width)
            key_part = lax.optimization_barrier(key_part.astype(jnp.bfloat16)).astype(jnp.float32)
            value_part = jnp.einsum('hqk,qhe->khe', probs_low, grad_block).reshape(window, feature_width)
            value_part = lax.optimization_barrier(value_part.astype(jnp.bfloat16)).astype(jnp.float32)
            current = lax.dynamic_slice_in_dim(key_acc, first, window, 0)
            key_acc = lax.dynamic_update_slice_in_dim(key_acc, current + key_part, first, 0)
            current = lax.dynamic_slice_in_dim(value_acc, first, window, 0)
            value_acc = lax.dynamic_update_slice_in_dim(value_acc, current + value_part, first, 0)
            return ((key_acc, value_acc), (attended.reshape(TOK_DEV, feature_width), query_part))
        start_acc = jnp.zeros((TOKENS + 2 * margin, feature_width), jnp.float32)
        (key_acc, value_acc), (attended_all, query_all) = lax.scan(one_block, (start_acc, start_acc), jnp.arange(block_count, dtype=jnp.int32))
        attended_all = attended_all.reshape(TOKENS, feature_width)
        weight_grad = weight_grad + jnp.dot(out_grad[pack_index].T, attended_all, preferred_element_type=jnp.float32)
        query_grads.append(query_all.reshape(TOKENS, feature_width))
        key_grads.append(key_acc[margin:margin + TOKENS].astype(jnp.bfloat16))
        value_grads.append(value_acc[margin:margin + TOKENS].astype(jnp.bfloat16))
    return (jnp.stack(query_grads, 0), jnp.stack(key_grads, 0), jnp.stack(value_grads, 0), weight_grad)
```

```python
import math

import jax
import jax.numpy as jnp
from jax import lax
from jax.experimental import pallas as pl
from jax.experimental.pallas import tpu as pltpu
from jax.sharding import Mesh, PartitionSpec as P

HEADS = 8
HEAD = 128
TOK = 128
CHIP = 2 * TOK
HALF = HEADS * HEAD // 2
REACH = 2
OFFSETS = tuple(range(-REACH, REACH + 1))
SUBS = 2 * len(OFFSETS)
SCALE = 1.0 / math.sqrt(HEAD)
SWAP = [(0, 1), (1, 0)]


def nt(a, b):
    return lax.dot_general(a, b, (((1,), (1,)), ((), ())), preferred_element_type=jnp.float32)


def nn(a, b):
    return lax.dot_general(a, b, (((1,), (0,)), ((), ())), preferred_element_type=jnp.float32)


def tn(a, b):
    return lax.dot_general(a, b, (((0,), (0,)), ((), ())), preferred_element_type=jnp.float32)


def block_base(info, sub):
    own = info[0]
    core = info[1]
    parity = core if sub % 2 == 0 else 1 - core
    return own + OFFSETS[sub // 2] * CHIP + parity * TOK


def needed(info, base):
    return jnp.logical_and(base < info[3], base + TOK > info[2])


def masked_scores(keys, query, spans, base):
    scores = nt(keys, query) * SCALE
    position = base + lax.broadcasted_iota(jnp.int32, (TOK, CHIP), 0)
    taken = jnp.logical_and(position >= spans[0:1, :], position < spans[1:2, :])
    return jnp.where(taken, scores, -1e30)


def forward_kernel(info, spans, query, *rest):
    windows = rest[: len(OFFSETS)]
    attended, log_norm, scores, peak, total, acc = rest[len(OFFSETS) :]
    peak[...] = jnp.full((1, CHIP), -1e30, jnp.float32)
    total[...] = jnp.zeros((1, CHIP), jnp.float32)
    acc[...] = jnp.zeros((HEAD, CHIP), jnp.float32)
    for sub in range(SUBS):
        base = block_base(info, sub)
        rows = pl.ds(sub % 2 * TOK, TOK)

        @pl.when(needed(info, base))
        def _(sub=sub, base=base, rows=rows):
            block = masked_scores(windows[sub // 2][0, rows, :], query[...], spans, base)
            scores[sub] = block
            peak[...] = jnp.maximum(peak[...], jnp.max(block, axis=0, keepdims=True))

    for sub in range(SUBS):
        base = block_base(info, sub)
        rows = pl.ds(sub % 2 * TOK, TOK)

        @pl.when(needed(info, base))
        def _(sub=sub, rows=rows):
            weights = jnp.exp(scores[sub] - peak[...])
            total[...] += jnp.sum(weights, axis=0, keepdims=True)
            acc[...] += tn(windows[sub // 2][1, rows, :], weights.astype(jnp.bfloat16))

    attended[...] = (acc[...] * (1.0 / total[...])).T.astype(jnp.bfloat16)
    log_norm[0] = peak[...] + jnp.log(total[...])


def backward_kernel(info, spans, query, attended, log_norm, out_grad, weight, *rest):
    windows = rest[: len(OFFSETS)]
    query_grad = rest[len(OFFSETS)]
    terms = rest[len(OFFSETS) + 1 : 2 * len(OFFSETS) + 1]
    grad_f32, acc = rest[2 * len(OFFSETS) + 1 :]
    grad = nn(out_grad[...], weight[0]).astype(jnp.bfloat16)
    grad_f32[...] = grad
    acc[...] = jnp.zeros((HEAD, CHIP), jnp.float32)
    product = grad.astype(jnp.float32) * attended[...].astype(jnp.float32)
    row_delta = jnp.sum(product.T, axis=0, keepdims=True)
    for sub in range(SUBS):
        base = block_base(info, sub)
        rows = pl.ds(sub % 2 * TOK, TOK)
        touched = needed(info, base)
        term = terms[sub // 2]

        @pl.when(touched)
        def _(sub=sub, base=base, rows=rows, term=term):
            keys = windows[sub // 2][0, rows, :]
            values = windows[sub // 2][1, rows, :]
            grad_low = grad_f32[...]
            probs = jnp.exp(masked_scores(keys, query[...], spans, base) - log_norm[0])
            dprobs = nt(values, grad_low)
            dscores = (probs * (dprobs - row_delta)).astype(jnp.bfloat16)
            acc[...] += tn(keys, dscores)
            term[0, rows, :] = (SCALE * nn(dscores, query[...])).astype(term.dtype)
            term[1, rows, :] = nn(probs.astype(jnp.bfloat16), grad_low).astype(term.dtype)

        @pl.when(jnp.logical_not(touched))
        def _(rows=rows, term=term):
            term[:, rows, :] = jnp.zeros((2, TOK, HEAD), term.dtype)

    query_grad[...] = (SCALE * acc[...]).T.astype(jnp.bfloat16)


def smem():
    return pl.BlockSpec(memory_space=pltpu.SMEM)


def whole(shape):
    return pl.BlockSpec(shape, lambda h: (0,) * len(shape))


def head_columns(rows):
    return pl.BlockSpec((rows, HEAD), lambda h: (0, h))


def window_spec():
    return pl.BlockSpec((2, CHIP, HEAD), lambda h: (0, 0, h))


def forward(info, spans, query, windows):
    return pl.pallas_call(
        forward_kernel,
        grid=(HEADS // 2,),
        in_specs=[smem(), whole((2, CHIP)), head_columns(CHIP)] + [window_spec() for _ in OFFSETS],
        out_specs=[head_columns(CHIP), pl.BlockSpec((1, 1, CHIP), lambda h: (h, 0, 0))],
        out_shape=[
            jax.ShapeDtypeStruct((CHIP, HALF), jnp.bfloat16),
            jax.ShapeDtypeStruct((HEADS // 2, 1, CHIP), jnp.float32),
        ],
        scratch_shapes=[
            pltpu.VMEM((SUBS, TOK, CHIP), jnp.float32),
            pltpu.VMEM((1, CHIP), jnp.float32),
            pltpu.VMEM((1, CHIP), jnp.float32),
            pltpu.VMEM((HEAD, CHIP), jnp.float32),
        ],
        compiler_params=pltpu.CompilerParams(vmem_limit_bytes=24 * 1024 * 1024),
        cost_estimate=pl.CostEstimate(
            flops=4 * HALF * CHIP * SUBS * TOK, bytes_accessed=4 * 1024 * 1024, transcendentals=0
        ),
        name="attended",
    )(info, spans, query, *windows)


def backward(info, spans, query, attended, log_norm, out_grad, weight, windows):
    features = out_grad.shape[1]
    return pl.pallas_call(
        backward_kernel,
        grid=(HEADS // 2,),
        in_specs=[
            smem(),
            whole((2, CHIP)),
            head_columns(CHIP),
            head_columns(CHIP),
            pl.BlockSpec((1, 1, CHIP), lambda h: (h, 0, 0)),
            whole((CHIP, features)),
            pl.BlockSpec((1, features, HEAD), lambda h: (h, 0, 0)),
        ]
        + [window_spec() for _ in OFFSETS],
        out_specs=[head_columns(CHIP)] + [window_spec() for _ in OFFSETS],
        out_shape=[jax.ShapeDtypeStruct((CHIP, HALF), jnp.bfloat16)]
        + [
            jax.ShapeDtypeStruct((2, CHIP, HALF), jnp.float32 if o == 0 else jnp.bfloat16)
            for o in OFFSETS
        ],
        scratch_shapes=[
            pltpu.VMEM((CHIP, HEAD), jnp.bfloat16),
            pltpu.VMEM((HEAD, CHIP), jnp.float32),
        ],
        compiler_params=pltpu.CompilerParams(vmem_limit_bytes=24 * 1024 * 1024),
        cost_estimate=pl.CostEstimate(
            flops=10 * HALF * CHIP * SUBS * TOK,
            bytes_accessed=8 * 1024 * 1024,
            transcendentals=0,
        ),
        name="gradients",
    )(info, spans, query, attended, log_norm, out_grad, weight, *windows)


def to_chip(block, distance):
    chips = lax.axis_size("y") * lax.axis_size("z")
    route = [(i, i + distance) for i in range(chips) if 0 <= i + distance < chips]
    return lax.ppermute(block, ("y", "z"), route)


def halves(core, matrix):
    own = lax.dynamic_slice_in_dim(matrix, core * HALF, HALF, matrix.ndim - 1)
    other = lax.dynamic_slice_in_dim(matrix, (1 - core) * HALF, HALF, matrix.ndim - 1)
    return own, other


def on_device(query, keys, values, out_grad, out_weight, lengths):
    core = lax.axis_index("c")
    along_x = lax.axis_index("x")
    chip = lax.axis_index("y") * lax.axis_size("z") + lax.axis_index("z")
    size_x, size_y, size_z = (lax.axis_size(a) for a in ("x", "y", "z"))
    features = out_grad.shape[2]

    own_kv, other_kv = halves(core, jnp.stack([keys[0], values[0]]))
    chip_kv = jnp.concatenate([own_kv, lax.ppermute(other_kv, "c", SWAP)], axis=1)
    windows = [chip_kv if o == 0 else to_chip(chip_kv, -o) for o in OFFSETS]
    own_query, other_query = halves(core, query[0])
    chip_query = jnp.concatenate([own_query, lax.ppermute(other_query, "c", SWAP)], axis=0)
    chip_grad = jnp.concatenate([out_grad[0], lax.ppermute(out_grad[0], "c", SWAP)], axis=0)

    rows = out_weight.shape[0]
    piece = lax.dynamic_index_in_dim(
        out_weight.reshape(rows, 2, size_x, HEAD), along_x, 2, keepdims=False
    )
    piece = jnp.broadcast_to(piece.transpose(1, 0, 2)[None], (size_z, 2, rows, HEAD))
    piece = lax.all_to_all(piece.reshape(2 * size_z, rows, HEAD), ("z", "c"), 0, 0)
    piece = piece.reshape(1, 2 * size_z * rows, HEAD)
    piece = jnp.broadcast_to(piece, (size_x * size_y,) + piece.shape[1:])
    weight = lax.all_to_all(piece, ("x", "y"), 0, 0).reshape(size_x, features, HEAD)

    ends = jnp.cumsum(lengths[0])
    starts = ends - lengths[0]
    place = jnp.arange(CHIP, dtype=jnp.int32)
    first = chip * CHIP
    positions = first + jnp.where(core == 0, place, (place + TOK) % CHIP)
    image_start = jnp.max(
        jnp.where(starts[:, None] <= positions[None, :], starts[:, None], 0), axis=0
    )
    image_end = jnp.min(
        jnp.where(ends[:, None] > positions[None, :], ends[:, None], jnp.int32(2**30)), axis=0
    )
    spans = jnp.stack([image_start, image_end])
    info = jnp.stack([first, core, jnp.min(image_start), jnp.max(image_end)]).astype(jnp.int32)

    attended, log_norm = forward(info, spans, chip_query, windows)

    partial = tn(chip_grad, attended).astype(jnp.bfloat16)
    partial = partial.reshape(size_x * size_y, features // (size_x * size_y), HALF)
    partial = lax.all_to_all(partial, ("x", "y"), 0, 0)
    partial = jnp.sum(partial.astype(jnp.float32), axis=0).astype(jnp.bfloat16)
    partial = partial.reshape(2 * size_z, -1, HALF)
    partial = lax.all_to_all(partial, ("z", "c"), 0, 0).reshape(size_z, 2, -1, HALF)
    partial = jnp.sum(partial.astype(jnp.float32), axis=0)
    weight_grad = jnp.concatenate([partial[0], partial[1]], axis=1)

    query_grad, *terms = backward(
        info, spans, chip_query, attended, log_norm, chip_grad, weight, windows
    )
    total = terms[REACH]
    for o, term in zip(OFFSETS, terms):
        if o != 0:
            total = total + to_chip(term, o).astype(jnp.float32)
    grads = jnp.concatenate([query_grad[None], total.astype(jnp.bfloat16)], axis=0)
    mine = grads[:, :TOK]
    theirs = lax.ppermute(grads[:, TOK:], "c", SWAP)
    low = jnp.where(core == 0, mine, theirs)
    high = jnp.where(core == 0, theirs, mine)
    grads = jnp.concatenate([low, high], axis=2)
    return (grads[0:1], grads[1:2], grads[2:3], weight_grad)


def solution(mesh):
    fine = Mesh(mesh.devices.reshape(4, 4, 8, 2), ("x", "y", "z", "c"))
    tokens = P("x", ("y", "z", "c"), None)
    return jax.shard_map(
        on_device,
        mesh=fine,
        in_specs=(tokens, tokens, tokens, tokens, P(("y", "z", "c"), None), P("x", None)),
        out_specs=(tokens, tokens, tokens, P(("x", "y", "z", "c"), None)),
        check_vma=False,
    )
```

```python
import math

import jax
import jax.numpy as jnp
from jax import lax
from jax.experimental import pallas as pl
from jax.experimental.pallas import tpu as pltpu
from jax.sharding import Mesh, PartitionSpec as P

HEADS = 8
HEAD = 128
TOK = 128
CHIP = 2 * TOK
HALF = HEADS * HEAD // 2
REACH = 2
OFFSETS = tuple(range(-REACH, REACH + 1))
SUBS = 2 * len(OFFSETS)
SCALE = 1.0 / math.sqrt(HEAD)
LOG2E = math.log2(math.e)
PER = 2
SWAP = [(0, 1), (1, 0)]


def nt(a, b):
    return lax.dot_general(a, b, (((1,), (1,)), ((), ())), preferred_element_type=jnp.float32)


def nn(a, b):
    return lax.dot_general(a, b, (((1,), (0,)), ((), ())), preferred_element_type=jnp.float32)


def tn(a, b):
    return lax.dot_general(a, b, (((0,), (0,)), ((), ())), preferred_element_type=jnp.float32)


def block_base(info, sub):
    own = info[0]
    core = info[1]
    parity = core if sub % 2 == 0 else 1 - core
    return own + OFFSETS[sub // 2] * CHIP + parity * TOK


def needed(info, base):
    return jnp.logical_and(base < info[3], base + TOK > info[2])


def block_mask(spans, base):
    position = base + lax.broadcasted_iota(jnp.int32, (TOK, CHIP), 0)
    return jnp.logical_and(position >= spans[0:1, :], position < spans[1:2, :])


def masked_scores(keys, query, taken):
    return jnp.where(taken, nt(keys, query) * (SCALE * LOG2E), -1e30)


def by_eights(block):
    return block.reshape(TOK // 8, 8, CHIP)


def forward_kernel(info, spans, query, *rest):
    windows = rest[: len(OFFSETS)]
    attended, log_norm, scores, peak, total, acc = rest[len(OFFSETS) :]
    peak[...] = jnp.full((PER, 8, CHIP), -1e30, jnp.float32)
    total[...] = jnp.zeros((PER, 8, CHIP), jnp.float32)
    acc[...] = jnp.zeros((PER, HEAD, CHIP), jnp.float32)
    heads = [(h, pl.ds(h * HEAD, HEAD)) for h in range(PER)]
    for sub in range(SUBS):
        base = block_base(info, sub)
        rows = pl.ds(sub % 2 * TOK, TOK)

        @pl.when(needed(info, base))
        def _(sub=sub, base=base, rows=rows):
            taken = block_mask(spans, base)
            for h, cols in heads:
                block = masked_scores(windows[sub // 2][0, rows, cols], query[:, cols], taken)
                scores[h, sub] = block
                peak[h] = jnp.maximum(peak[h], jnp.max(by_eights(block), axis=0))

    for h, cols in heads:
        peak[h] = jnp.broadcast_to(jnp.max(peak[h], axis=0, keepdims=True), (8, CHIP))
    for sub in range(SUBS):
        base = block_base(info, sub)
        rows = pl.ds(sub % 2 * TOK, TOK)

        @pl.when(needed(info, base))
        def _(sub=sub, rows=rows):
            for h, cols in heads:
                weights = jnp.exp2(scores[h, sub] - peak[h, 0:1, :])
                total[h] += jnp.sum(by_eights(weights), axis=0)
                acc[h] += tn(windows[sub // 2][1, rows, cols], weights.astype(jnp.bfloat16))

    for h, cols in heads:
        row_total = jnp.sum(total[h], axis=0, keepdims=True)
        attended[:, cols] = (acc[h] * (1.0 / row_total)).T.astype(jnp.bfloat16)
        log_norm[h] = peak[h, 0:1, :] + jnp.log(row_total) * LOG2E


def backward_kernel(info, spans, query, attended, log_norm, out_grad, weight, *rest):
    windows = rest[: len(OFFSETS)]
    query_grad = rest[len(OFFSETS)]
    terms = rest[len(OFFSETS) + 1 : 2 * len(OFFSETS) + 1]
    grad, row_delta, acc = rest[2 * len(OFFSETS) + 1 :]
    heads = [(h, pl.ds(h * HEAD, HEAD)) for h in range(PER)]
    acc[...] = jnp.zeros((PER, HEAD, CHIP), jnp.float32)
    for h, cols in heads:
        grad[h] = nn(out_grad[...], weight[h]).astype(jnp.bfloat16)
        product = grad[h].astype(jnp.float32) * attended[:, cols].astype(jnp.float32)
        row_delta[h] = jnp.sum(product.T, axis=0, keepdims=True)
    for sub in range(SUBS):
        base = block_base(info, sub)
        rows = pl.ds(sub % 2 * TOK, TOK)
        touched = needed(info, base)
        term = terms[sub // 2]

        @pl.when(touched)
        def _(sub=sub, base=base, rows=rows, term=term):
            taken = block_mask(spans, base)
            for h, cols in heads:
                keys = windows[sub // 2][0, rows, cols]
                values = windows[sub // 2][1, rows, cols]
                probs = jnp.exp2(masked_scores(keys, query[:, cols], taken) - log_norm[h])
                dprobs = nt(values, grad[h])
                dscores = (probs * (dprobs - row_delta[h])).astype(jnp.bfloat16)
                acc[h] += tn(keys, dscores)
                term[0, rows, cols] = (SCALE * nn(dscores, query[:, cols])).astype(term.dtype)
                term[1, rows, cols] = nn(probs.astype(jnp.bfloat16), grad[h]).astype(term.dtype)

        @pl.when(jnp.logical_not(touched))
        def _(rows=rows, term=term):
            term[:, rows, :] = jnp.zeros((2, TOK, PER * HEAD), term.dtype)

    for h, cols in heads:
        query_grad[:, cols] = (SCALE * acc[h]).T.astype(jnp.bfloat16)


def smem():
    return pl.BlockSpec(memory_space=pltpu.SMEM)


def whole(shape):
    return pl.BlockSpec(shape, lambda h: (0,) * len(shape))


def head_columns(rows):
    return pl.BlockSpec((rows, PER * HEAD), lambda h: (0, h))


def head_rows(*shape):
    return pl.BlockSpec((PER,) + shape, lambda h: (h, 0, 0))


def window_spec():
    return pl.BlockSpec((2, CHIP, PER * HEAD), lambda h: (0, 0, h))


def forward(info, spans, query, windows):
    return pl.pallas_call(
        forward_kernel,
        grid=(HEADS // 2 // PER,),
        in_specs=[smem(), whole((2, CHIP)), head_columns(CHIP)] + [window_spec() for _ in OFFSETS],
        out_specs=[head_columns(CHIP), head_rows(1, CHIP)],
        out_shape=[
            jax.ShapeDtypeStruct((CHIP, HALF), jnp.bfloat16),
            jax.ShapeDtypeStruct((HEADS // 2, 1, CHIP), jnp.float32),
        ],
        scratch_shapes=[
            pltpu.VMEM((PER, SUBS, TOK, CHIP), jnp.float32),
            pltpu.VMEM((PER, 8, CHIP), jnp.float32),
            pltpu.VMEM((PER, 8, CHIP), jnp.float32),
            pltpu.VMEM((PER, HEAD, CHIP), jnp.float32),
        ],
        compiler_params=pltpu.CompilerParams(vmem_limit_bytes=32 * 1024 * 1024),
        cost_estimate=pl.CostEstimate(
            flops=4 * HALF * CHIP * SUBS * TOK, bytes_accessed=8 * 1024 * 1024, transcendentals=0
        ),
        name="attended",
    )(info, spans, query, *windows)


def backward(info, spans, query, attended, log_norm, out_grad, weight, windows):
    features = out_grad.shape[1]
    return pl.pallas_call(
        backward_kernel,
        grid=(HEADS // 2 // PER,),
        in_specs=[
            smem(),
            whole((2, CHIP)),
            head_columns(CHIP),
            head_columns(CHIP),
            head_rows(1, CHIP),
            whole((CHIP, features)),
            head_rows(features, HEAD),
        ]
        + [window_spec() for _ in OFFSETS],
        out_specs=[head_columns(CHIP)] + [window_spec() for _ in OFFSETS],
        out_shape=[jax.ShapeDtypeStruct((CHIP, HALF), jnp.bfloat16)]
        + [
            jax.ShapeDtypeStruct((2, CHIP, HALF), jnp.float32 if abs(o) < REACH else jnp.bfloat16)
            for o in OFFSETS
        ],
        scratch_shapes=[
            pltpu.VMEM((PER, CHIP, HEAD), jnp.bfloat16),
            pltpu.VMEM((PER, 1, CHIP), jnp.float32),
            pltpu.VMEM((PER, HEAD, CHIP), jnp.float32),
        ],
        compiler_params=pltpu.CompilerParams(vmem_limit_bytes=32 * 1024 * 1024),
        cost_estimate=pl.CostEstimate(
            flops=10 * HALF * CHIP * SUBS * TOK,
            bytes_accessed=16 * 1024 * 1024,
            transcendentals=0,
        ),
        name="gradients",
    )(info, spans, query, attended, log_norm, out_grad, weight, *windows)


def to_chip(block, distance):
    chips = lax.axis_size("y") * lax.axis_size("z")
    route = [(i, i + distance) for i in range(chips) if 0 <= i + distance < chips]
    return lax.ppermute(block, ("y", "z"), route)


def halves(core, matrix):
    own = lax.dynamic_slice_in_dim(matrix, core * HALF, HALF, matrix.ndim - 1)
    other = lax.dynamic_slice_in_dim(matrix, (1 - core) * HALF, HALF, matrix.ndim - 1)
    return own, other


def on_device(query, keys, values, out_grad, out_weight, lengths):
    core = lax.axis_index("c")
    along_x = lax.axis_index("x")
    chip = lax.axis_index("y") * lax.axis_size("z") + lax.axis_index("z")
    size_x, size_y, size_z = (lax.axis_size(a) for a in ("x", "y", "z"))
    features = out_grad.shape[2]

    own_kv, other_kv = halves(core, jnp.stack([keys[0], values[0]]))
    chip_kv = jnp.concatenate([own_kv, lax.ppermute(other_kv, "c", SWAP)], axis=1)
    chip_kv, out_weight = lax.optimization_barrier((chip_kv, out_weight))
    below = to_chip(chip_kv, 1)
    above = to_chip(chip_kv, -1)
    windows = [to_chip(below, 1), below, chip_kv, above, to_chip(above, -1)]
    own_query, other_query = halves(core, query[0])
    chip_query = jnp.concatenate([own_query, lax.ppermute(other_query, "c", SWAP)], axis=0)
    chip_grad = jnp.concatenate([out_grad[0], lax.ppermute(out_grad[0], "c", SWAP)], axis=0)

    rows = out_weight.shape[0]
    piece = lax.dynamic_index_in_dim(
        out_weight.reshape(rows, 2, size_x, HEAD), along_x, 2, keepdims=False
    )
    piece = jnp.broadcast_to(piece.transpose(1, 0, 2)[None], (size_z, 2, rows, HEAD))
    piece = lax.all_to_all(piece.reshape(2 * size_z, rows, HEAD), ("z", "c"), 0, 0)
    piece = piece.reshape(1, 2 * size_z * rows, HEAD)
    piece = jnp.broadcast_to(piece, (size_x * size_y,) + piece.shape[1:])
    weight = lax.all_to_all(piece, ("x", "y"), 0, 0).reshape(size_x, features, HEAD)

    ends = jnp.cumsum(lengths[0])
    starts = ends - lengths[0]
    place = jnp.arange(CHIP, dtype=jnp.int32)
    first = chip * CHIP
    positions = first + jnp.where(core == 0, place, (place + TOK) % CHIP)
    image_start = jnp.max(
        jnp.where(starts[:, None] <= positions[None, :], starts[:, None], 0), axis=0
    )
    image_end = jnp.min(
        jnp.where(ends[:, None] > positions[None, :], ends[:, None], jnp.int32(2**30)), axis=0
    )
    spans = jnp.stack([image_start, image_end])
    info = jnp.stack([first, core, jnp.min(image_start), jnp.max(image_end)]).astype(jnp.int32)

    attended, log_norm = forward(info, spans, chip_query, windows)

    partial = tn(chip_grad, attended).astype(jnp.bfloat16)
    for axis, size in (("x", size_x), ("y", size_y)):
        partial = lax.all_to_all(partial.reshape(size, -1, HALF), axis, 0, 0)
        partial = jnp.sum(partial.astype(jnp.float32), axis=0).astype(jnp.bfloat16)
    partial = partial.reshape(2 * size_z, -1, HALF)
    partial = lax.all_to_all(partial, ("z", "c"), 0, 0).reshape(size_z, 2, -1, HALF)
    partial = jnp.sum(partial.astype(jnp.float32), axis=0)
    weight_grad = jnp.concatenate([partial[0], partial[1]], axis=1)

    query_grad, *terms = backward(
        info, spans, chip_query, attended, log_norm, chip_grad, weight, windows
    )
    total = terms[REACH]
    for side in (1, -1):
        passing = to_chip(terms[REACH + 2 * side], side).astype(jnp.float32)
        passing = (passing + terms[REACH + side]).astype(jnp.bfloat16)
        total = total + to_chip(passing, side).astype(jnp.float32)
    grads = jnp.concatenate([query_grad[None], total.astype(jnp.bfloat16)], axis=0)
    mine = grads[:, :TOK]
    theirs = lax.ppermute(grads[:, TOK:], "c", SWAP)
    low = jnp.where(core == 0, mine, theirs)
    high = jnp.where(core == 0, theirs, mine)
    grads = jnp.concatenate([low, high], axis=2)
    return (grads[0:1], grads[1:2], grads[2:3], weight_grad)


def solution(mesh):
    fine = Mesh(mesh.devices.reshape(4, 4, 8, 2), ("x", "y", "z", "c"))
    tokens = P("x", ("y", "z", "c"), None)
    return jax.shard_map(
        on_device,
        mesh=fine,
        in_specs=(tokens, tokens, tokens, tokens, P(("y", "z", "c"), None), P("x", None)),
        out_specs=(tokens, tokens, tokens, P(("x", "y", "z", "c"), None)),
        check_vma=False,
    )
```

```python
import math

import jax
import jax.numpy as jnp
from jax import lax
from jax.experimental import pallas as pl
from jax.experimental.pallas import tpu as pltpu
from jax.sharding import Mesh, PartitionSpec as P

HEADS = 8
HEAD = 128
TOK = 128
CHIP = 2 * TOK
MINE = HEADS // 2
HALF = MINE * HEAD
NEAR = (-1, 0, 1)
FAR = (-2, 2)
SCALE = 1.0 / math.sqrt(HEAD)
LOG2E = math.log2(math.e)
GRAD_PARTS = 0
NEAR_FORWARD = 2013265920
FAR_FORWARD = 2684354560
FAR_BACKWARD = 0
NEAR_BACKWARD = 0
SWAP = [(0, 1), (1, 0)]
COLUMNS = [(h, slice(h * HEAD, (h + 1) * HEAD)) for h in range(MINE)]


def nt(a, b):
    return lax.dot_general(a, b, (((1,), (1,)), ((), ())), preferred_element_type=jnp.float32)


def nn(a, b):
    return lax.dot_general(a, b, (((1,), (0,)), ((), ())), preferred_element_type=jnp.float32)


def tn(a, b):
    return lax.dot_general(a, b, (((0,), (0,)), ((), ())), preferred_element_type=jnp.float32)


def key_blocks(info, offsets, body, other=None):
    for slot, offset in enumerate(offsets):
        for half in range(2):
            parity = info[1] if half == 0 else 1 - info[1]
            base = info[0] + offset * CHIP + parity * TOK
            rows = slice(half * TOK, (half + 1) * TOK)
            needed = jnp.logical_and(base < info[3], base + TOK > info[2])

            @pl.when(needed)
            def _(slot=slot, half=half, rows=rows, base=base):
                body(slot, 2 * slot + half, rows, base)

            if other is not None:

                @pl.when(jnp.logical_not(needed))
                def _(slot=slot, rows=rows):
                    other(slot, rows)


def block_mask(spans, base):
    position = base + lax.broadcasted_iota(jnp.int32, (TOK, CHIP), 0)
    return jnp.logical_and(position >= spans[0:1, :], position < spans[1:2, :])


def masked_scores(keys, query, taken):
    return jnp.where(taken, nt(keys, query) * (SCALE * LOG2E), -1e30)


def by_eights(block):
    return block.reshape(TOK // 8, 8, CHIP)


def over_eights(op, rows):
    return jnp.broadcast_to(op(rows, axis=0, keepdims=True), (8, CHIP))


def score_blocks(info, spans, query, offsets, windows, scores, peak):
    def body(slot, index, rows, base):
        taken = block_mask(spans, base)
        for h, cols in COLUMNS:
            block = masked_scores(windows[slot][0, rows, cols], query[:, cols], taken)
            scores[h, index] = block
            peak[h] = jnp.maximum(peak[h], jnp.max(by_eights(block), axis=0))

    key_blocks(info, offsets, body)
    for h, _ in COLUMNS:
        peak[h] = over_eights(jnp.max, peak[h])


def absorb_blocks(info, offsets, windows, scores, peak, total, acc):
    def body(slot, index, rows, base):
        for h, cols in COLUMNS:
            weights = jnp.exp2(scores[h, index] - peak[h, 0:1, :])
            total[h] += jnp.sum(by_eights(weights), axis=0)
            acc[h] += tn(windows[slot][1, rows, cols], weights.astype(jnp.bfloat16))

    key_blocks(info, offsets, body)


def near_forward_kernel(info, spans, query, below, own, above, peak, total, acc, scores):
    windows = (below, own, above)
    peak[...] = jnp.full(peak.shape, -1e30, jnp.float32)
    total[...] = jnp.zeros(total.shape, jnp.float32)
    acc[...] = jnp.zeros(acc.shape, jnp.float32)
    score_blocks(info, spans, query, NEAR, windows, scores, peak)
    absorb_blocks(info, NEAR, windows, scores, peak, total, acc)


def far_forward_kernel(
    info, spans, query, below, above, near_peak, near_total, near_acc,
    attended, log_norm, scores, peak, total, acc,
):
    windows = (below, above)
    peak[...] = near_peak[...]
    score_blocks(info, spans, query, FAR, windows, scores, peak)
    for h, _ in COLUMNS:
        shrink = jnp.exp2(near_peak[h] - peak[h])
        total[h] = near_total[h] * shrink
        acc[h] = near_acc[h] * shrink[0:1, :]
    absorb_blocks(info, FAR, windows, scores, peak, total, acc)
    for h, cols in COLUMNS:
        row_total = jnp.sum(total[h], axis=0, keepdims=True)
        attended[:, cols] = (acc[h] * (1.0 / row_total)).T.astype(jnp.bfloat16)
        log_norm[h] = peak[h, 0:1, :] + jnp.log(row_total) * LOG2E


def gradient_blocks(
    info, spans, query, grad, log_norm, row_delta, offsets, windows, acc, terms
):
    def body(slot, index, rows, base):
        taken = block_mask(spans, base)
        term = terms[slot]
        for h, cols in COLUMNS:
            keys = windows[slot][0, rows, cols]
            values = windows[slot][1, rows, cols]
            probs = jnp.exp2(masked_scores(keys, query[:, cols], taken) - log_norm[h])
            dprobs = nt(values, grad[:, cols])
            dscores = (probs * (dprobs - row_delta[h])).astype(jnp.bfloat16)
            acc[h] += tn(keys, dscores)
            term[0, rows, cols] = (SCALE * nn(dscores, query[:, cols])).astype(term.dtype)
            term[1, rows, cols] = nn(probs.astype(jnp.bfloat16), grad[:, cols]).astype(term.dtype)

    def other(slot, rows):
        terms[slot][:, rows, :] = jnp.zeros((2, TOK, HALF), terms[slot].dtype)

    key_blocks(info, offsets, body, other)


def grad_parts_kernel(info, own, other, weight, *rest):
    parts = rest[:-1]
    columns = rest[-1]
    for h, cols in COLUMNS:
        columns[:, cols] = weight[h]
    for slot, part in enumerate(parts):
        part[0:TOK, :] = nn(own[slot], columns[...]).astype(jnp.bfloat16)
        part[TOK:CHIP, :] = nn(other[slot], columns[...]).astype(jnp.bfloat16)


def far_backward_kernel(
    info, spans, query, attended, log_norm, below, above, *rest
):
    parts = rest[:-5]
    grad, row_delta, acc, term_below, term_above = rest[-5:]
    acc[...] = jnp.zeros(acc.shape, jnp.float32)
    for h, cols in COLUMNS:
        total = parts[0][:, cols].astype(jnp.float32)
        for part in parts[1:]:
            total = total + part[:, cols].astype(jnp.float32)
        head_grad = total.astype(jnp.bfloat16)
        grad[:, cols] = head_grad
        product = head_grad.astype(jnp.float32) * attended[:, cols].astype(jnp.float32)
        row_delta[h] = jnp.sum(product.T, axis=0, keepdims=True)
    gradient_blocks(
        info, spans, query, grad, log_norm, row_delta, FAR,
        (below, above), acc, (term_below, term_above),
    )


def near_backward_kernel(
    info, spans, query, log_norm, grad, row_delta, far_acc, below, own, above,
    query_grad, term_below, term_own, term_above, acc,
):
    acc[...] = far_acc[...]
    gradient_blocks(
        info, spans, query, grad, log_norm, row_delta, NEAR,
        (below, own, above), acc, (term_below, term_own, term_above),
    )
    for h, cols in COLUMNS:
        query_grad[:, cols] = (SCALE * acc[h]).T.astype(jnp.bfloat16)


def f32(*shape):
    return jax.ShapeDtypeStruct(shape, jnp.float32)


def bf16(*shape):
    return jax.ShapeDtypeStruct(shape, jnp.bfloat16)


EIGHTS = (MINE, 8, CHIP)
ROWS = (MINE, 1, CHIP)
SUMS = (MINE, HEAD, CHIP)
WINDOW = (2, CHIP, HALF)


def kernel(body, name, out_shape, scratch, flops, *operands):
    specs = [pl.BlockSpec(memory_space=pltpu.SMEM)]
    specs += [pl.BlockSpec(memory_space=pltpu.VMEM)] * (len(operands) - 1)
    return pl.pallas_call(
        body,
        in_specs=specs,
        out_specs=[pl.BlockSpec(memory_space=pltpu.VMEM)] * len(out_shape),
        out_shape=out_shape,
        scratch_shapes=[pltpu.VMEM(shape.shape, shape.dtype) for shape in scratch],
        compiler_params=pltpu.CompilerParams(vmem_limit_bytes=16 * 1024 * 1024),
        cost_estimate=pl.CostEstimate(flops=flops, bytes_accessed=0, transcendentals=0),
        name=name,
    )(*operands)


def to_chip(block, distance):
    chips = lax.axis_size("y") * lax.axis_size("z")
    route = [(i, i + distance) for i in range(chips) if 0 <= i + distance < chips]
    return lax.ppermute(block, ("y", "z"), route)


def along(axis, block, distance):
    size = lax.axis_size(axis)
    return lax.ppermute(block, axis, [(i, (i + distance) % size) for i in range(size)])


def swapped(block):
    return lax.ppermute(block, "c", SWAP)


def halves(core, matrix):
    own = lax.dynamic_slice_in_dim(matrix, core * HALF, HALF, matrix.ndim - 1)
    other = lax.dynamic_slice_in_dim(matrix, (1 - core) * HALF, HALF, matrix.ndim - 1)
    return own, other


def image_spans(lengths, core, first):
    ends = jnp.cumsum(lengths)
    starts = ends - lengths
    place = jnp.arange(CHIP, dtype=jnp.int32)
    positions = first + jnp.where(core == 0, place, (place + TOK) % CHIP)
    begun = starts[:, None] <= positions[None, :]
    open_ = ends[:, None] > positions[None, :]
    start = jnp.max(jnp.where(begun, starts[:, None], 0), axis=0)
    end = jnp.min(jnp.where(open_, ends[:, None], jnp.int32(2**30)), axis=0)
    info = jnp.stack([first, core, jnp.min(start), jnp.max(end)]).astype(jnp.int32)
    return info, jnp.stack([start, end])


def on_device(query, keys, values, out_grad, out_weight, lengths):
    core = lax.axis_index("c")
    x, y = lax.axis_index("x"), lax.axis_index("y")
    chip = y * lax.axis_size("z") + lax.axis_index("z")
    size_x, size_y, size_z = (lax.axis_size(a) for a in ("x", "y", "z"))
    quarter = out_grad.shape[2] // size_y

    own_kv, other_kv = halves(core, jnp.stack([keys[0], values[0]]))
    own = jnp.concatenate([own_kv, swapped(other_kv)], axis=1)
    below = to_chip(own, 1)
    above = to_chip(own, -1)

    own_query, other_query = halves(core, query[0])
    chip_query = jnp.concatenate([own_query, swapped(other_query)], axis=0)
    info, spans = image_spans(lengths[0], core, chip * CHIP)

    def quarters(axis, place):
        def piece(distance):
            start = (place + distance) % lax.axis_size(axis) * quarter
            return lax.dynamic_slice_in_dim(out_grad[0], start, quarter, 1)

        got = [piece(0)]
        got += [along(axis, piece(d), d) for d in range(1, lax.axis_size(axis))]
        got = jnp.stack(got)
        return got, swapped(got)

    mine, others = quarters("y", y)

    rows = out_weight.shape[0]
    piece = lax.dynamic_index_in_dim(
        out_weight.reshape(rows, 2, size_x, HEAD), x, 2, keepdims=False
    )
    piece = jnp.broadcast_to(piece.transpose(1, 0, 2)[None], (size_z, 2, rows, HEAD))
    piece = lax.all_to_all(piece.reshape(2 * size_z, rows, HEAD), ("z", "c"), 0, 0)
    piece = jnp.broadcast_to(piece.reshape(1, quarter, HEAD), (size_x, quarter, HEAD))
    weight = lax.all_to_all(piece, "x", 0, 0)

    parts = kernel(
        grad_parts_kernel, "grad_parts", [bf16(CHIP, HALF)] * size_y,
        [bf16(quarter, HALF)], GRAD_PARTS, info, mine, others, weight,
    )
    parts = [parts[0]] + [along("y", parts[d], -d) for d in range(1, size_y)]
    rows_grad = jnp.stack(quarters("x", x), axis=1).reshape(size_x * CHIP, quarter).T

    below, above, info, spans, chip_query = lax.optimization_barrier(
        (below, above, info, spans, chip_query)
    )
    far_below = to_chip(below, 1)
    far_above = to_chip(above, -1)

    near = kernel(
        near_forward_kernel, "near_forward", [f32(*EIGHTS), f32(*EIGHTS), f32(*SUMS)],
        [f32(MINE, 2 * len(NEAR), TOK, CHIP)], NEAR_FORWARD,
        info, spans, chip_query, below, own, above,
    )
    near, rows_grad = lax.optimization_barrier((near, rows_grad))
    attended, log_norm = kernel(
        far_forward_kernel, "far_forward", [bf16(CHIP, HALF), f32(*ROWS)],
        [f32(MINE, 2 * len(FAR), TOK, CHIP), f32(*EIGHTS), f32(*EIGHTS), f32(*SUMS)], FAR_FORWARD,
        info, spans, chip_query, far_below, far_above, *near,
    )
    attended_along = [attended] + [along("x", attended, d) for d in range(1, size_x)]

    grad, row_delta, far_acc, term_far_below, term_far_above = kernel(
        far_backward_kernel, "far_backward",
        [bf16(CHIP, HALF), f32(*ROWS), f32(*SUMS), bf16(*WINDOW), bf16(*WINDOW)],
        [], FAR_BACKWARD,
        info, spans, chip_query, attended, log_norm, far_below, far_above, *parts,
    )
    passed_below = to_chip(term_far_below, -1)
    passed_above = to_chip(term_far_above, 1)
    partial = nn(rows_grad, jnp.concatenate(attended_along, axis=0)).astype(jnp.bfloat16)
    partial, grad = lax.optimization_barrier((partial, grad))
    query_grad, term_below, term_own, term_above = kernel(
        near_backward_kernel, "near_backward",
        [bf16(CHIP, HALF), bf16(*WINDOW), f32(*WINDOW), bf16(*WINDOW)],
        [f32(*SUMS)], NEAR_BACKWARD,
        info, spans, chip_query, log_norm, grad, row_delta, far_acc, below, own, above,
    )
    partial = partial.reshape(size_y, -1, HALF)
    summed = 0.0
    for d in range(size_y):
        piece = lax.dynamic_index_in_dim(partial, (y + d) % size_y, 0, keepdims=False)
        summed = summed + (along("y", piece, d) if d else piece).astype(jnp.float32)
    partial = summed.astype(jnp.bfloat16)
    partial = lax.all_to_all(partial.reshape(2 * size_z, -1, HALF), ("z", "c"), 0, 0)
    partial = jnp.sum(partial.reshape(size_z, 2, -1, HALF).astype(jnp.float32), axis=0)
    weight_grad = jnp.concatenate([partial[0], partial[1]], axis=1)

    total = term_own
    for term, passed, side in ((term_below, passed_below, -1), (term_above, passed_above, 1)):
        both = (term.astype(jnp.float32) + passed.astype(jnp.float32)).astype(jnp.bfloat16)
        total = total + to_chip(both, side).astype(jnp.float32)
    grads = jnp.concatenate([query_grad[None], total.astype(jnp.bfloat16)], axis=0)
    stay = grads[:, :TOK]
    theirs = swapped(grads[:, TOK:])
    low = jnp.where(core == 0, stay, theirs)
    high = jnp.where(core == 0, theirs, stay)
    grads = jnp.concatenate([low, high], axis=2)
    return (grads[0:1], grads[1:2], grads[2:3], weight_grad)


def solution(mesh):
    fine = Mesh(mesh.devices.reshape(4, 4, 8, 2), ("x", "y", "z", "c"))
    tokens = P("x", ("y", "z", "c"), None)
    return jax.shard_map(
        on_device,
        mesh=fine,
        in_specs=(tokens, tokens, tokens, tokens, P(("y", "z", "c"), None), P("x", None)),
        out_specs=(tokens, tokens, tokens, P(("x", "y", "z", "c"), None)),
        check_vma=False,
    )
```

```python
import math

import jax
import jax.numpy as jnp
from jax import lax
from jax.experimental import pallas as pl
from jax.experimental.pallas import tpu as pltpu
from jax.sharding import Mesh, PartitionSpec as P

HEADS = 8
HEAD = 128
TOK = 128
CHIP = 2 * TOK
MINE = HEADS // 2
HALF = MINE * HEAD
NEAR = (-1, 0, 1)
FAR = (-2, 2)
SCALE = 1.0 / math.sqrt(HEAD)
LOG2E = math.log2(math.e)
GRAD_PARTS = 0
NEAR_FORWARD = 2013265920
FAR_FORWARD = 2684354560
FAR_BACKWARD = 0
NEAR_BACKWARD = 0
SWAP = [(0, 1), (1, 0)]
COLUMNS = [(h, slice(h * HEAD, (h + 1) * HEAD)) for h in range(MINE)]


def nt(a, b):
    return lax.dot_general(a, b, (((1,), (1,)), ((), ())), preferred_element_type=jnp.float32)


def nn(a, b):
    return lax.dot_general(a, b, (((1,), (0,)), ((), ())), preferred_element_type=jnp.float32)


def tn(a, b):
    return lax.dot_general(a, b, (((0,), (0,)), ((), ())), preferred_element_type=jnp.float32)


def key_blocks(info, offsets, body, other=None):
    for slot, offset in enumerate(offsets):
        for half in range(2):
            parity = info[1] if half == 0 else 1 - info[1]
            base = info[0] + offset * CHIP + parity * TOK
            rows = slice(half * TOK, (half + 1) * TOK)
            needed = jnp.logical_and(base < info[3], base + TOK > info[2])

            @pl.when(needed)
            def _(slot=slot, half=half, rows=rows, base=base):
                body(slot, 2 * slot + half, rows, base)

            if other is not None:

                @pl.when(jnp.logical_not(needed))
                def _(slot=slot, rows=rows):
                    other(slot, rows)


def block_mask(spans, base):
    position = base + lax.broadcasted_iota(jnp.int32, (TOK, CHIP), 0)
    return jnp.logical_and(position >= spans[0:1, :], position < spans[1:2, :])


def masked_scores(keys, query, taken):
    return jnp.where(taken, nt(keys, query) * (SCALE * LOG2E), -1e30)


def by_eights(block):
    return block.reshape(TOK // 8, 8, CHIP)


def over_eights(op, rows):
    return jnp.broadcast_to(op(rows, axis=0, keepdims=True), (8, CHIP))


def score_blocks(info, spans, query, offsets, windows, scores, peak):
    def body(slot, index, rows, base):
        taken = block_mask(spans, base)
        for h, cols in COLUMNS:
            block = masked_scores(windows[slot][0, rows, cols], query[:, cols], taken)
            scores[h, index] = block
            peak[h] = jnp.maximum(peak[h], jnp.max(by_eights(block), axis=0))

    key_blocks(info, offsets, body)
    for h, _ in COLUMNS:
        peak[h] = over_eights(jnp.max, peak[h])


def absorb_blocks(info, offsets, windows, scores, peak, total, acc):
    def body(slot, index, rows, base):
        for h, cols in COLUMNS:
            weights = jnp.exp2(scores[h, index] - peak[h, 0:1, :])
            total[h] += jnp.sum(by_eights(weights), axis=0)
            acc[h] += tn(windows[slot][1, rows, cols], weights.astype(jnp.bfloat16))

    key_blocks(info, offsets, body)


def spans_kernel(place, lengths, spans, info):
    first, core = place[0], place[1]
    index = lax.broadcasted_iota(jnp.int32, (1, CHIP), 1)
    swapped_index = jnp.where(index < TOK, index + TOK, index - TOK)
    positions = first + jnp.where(core == 0, index, swapped_index)
    start = jnp.zeros((1, CHIP), jnp.int32)
    end = jnp.zeros((1, CHIP), jnp.int32)
    begin, low, high = jnp.int32(0), jnp.int32(0), jnp.int32(0)
    for image in range(lengths.shape[1]):
        finish = begin + lengths[0, image]
        begun = positions >= begin
        start = jnp.where(begun, begin, start)
        end = jnp.where(begun, finish, end)
        low = jnp.where(first >= begin, begin, low)
        high = jnp.where(first + CHIP - 1 >= begin, finish, high)
        begin = finish
    spans[0:1, :] = start
    spans[1:2, :] = end
    info[0] = first
    info[1] = core
    info[2] = low
    info[3] = high


def near_forward_kernel(info, spans, query, below, own, above, peak, total, acc, scores):
    windows = (below, own, above)
    peak[...] = jnp.full(peak.shape, -1e30, jnp.float32)
    total[...] = jnp.zeros(total.shape, jnp.float32)
    acc[...] = jnp.zeros(acc.shape, jnp.float32)
    score_blocks(info, spans, query, NEAR, windows, scores, peak)
    absorb_blocks(info, NEAR, windows, scores, peak, total, acc)


def far_forward_kernel(
    info, spans, query, below, above, near_peak, near_total, near_acc,
    attended, log_norm, scores, peak, total, acc,
):
    windows = (below, above)
    peak[...] = near_peak[...]
    score_blocks(info, spans, query, FAR, windows, scores, peak)
    for h, _ in COLUMNS:
        shrink = jnp.exp2(near_peak[h] - peak[h])
        total[h] = near_total[h] * shrink
        acc[h] = near_acc[h] * shrink[0:1, :]
    absorb_blocks(info, FAR, windows, scores, peak, total, acc)
    for h, cols in COLUMNS:
        row_total = jnp.sum(total[h], axis=0, keepdims=True)
        attended[:, cols] = (acc[h] * (1.0 / row_total)).T.astype(jnp.bfloat16)
        log_norm[h] = peak[h, 0:1, :] + jnp.log(row_total) * LOG2E


def gradient_blocks(
    info, spans, query, grad, log_norm, row_delta, offsets, windows, acc, terms
):
    def body(slot, index, rows, base):
        taken = block_mask(spans, base)
        term = terms[slot]
        for h, cols in COLUMNS:
            keys = windows[slot][0, rows, cols]
            values = windows[slot][1, rows, cols]
            probs = jnp.exp2(masked_scores(keys, query[:, cols], taken) - log_norm[h])
            dprobs = nt(values, grad[:, cols])
            dscores = (probs * (dprobs - row_delta[h])).astype(jnp.bfloat16)
            acc[h] += tn(keys, dscores)
            term[0, rows, cols] = (SCALE * nn(dscores, query[:, cols])).astype(term.dtype)
            term[1, rows, cols] = nn(probs.astype(jnp.bfloat16), grad[:, cols]).astype(term.dtype)

    def other(slot, rows):
        terms[slot][:, rows, :] = jnp.zeros((2, TOK, HALF), terms[slot].dtype)

    key_blocks(info, offsets, body, other)


def grad_parts_kernel(info, own, other, weight, *rest):
    parts = rest[:-1]
    columns = rest[-1]
    for h, cols in COLUMNS:
        columns[:, cols] = weight[h]
    for slot, part in enumerate(parts):
        part[0:TOK, :] = nn(own[slot], columns[...]).astype(jnp.bfloat16)
        part[TOK:CHIP, :] = nn(other[slot], columns[...]).astype(jnp.bfloat16)


def far_backward_kernel(
    info, spans, query, attended, log_norm, below, above, *rest
):
    parts = rest[:-5]
    grad, row_delta, acc, term_below, term_above = rest[-5:]
    acc[...] = jnp.zeros(acc.shape, jnp.float32)
    for h, cols in COLUMNS:
        total = parts[0][:, cols].astype(jnp.float32)
        for part in parts[1:]:
            total = total + part[:, cols].astype(jnp.float32)
        head_grad = total.astype(jnp.bfloat16)
        grad[:, cols] = head_grad
        product = head_grad.astype(jnp.float32) * attended[:, cols].astype(jnp.float32)
        row_delta[h] = jnp.sum(product.T, axis=0, keepdims=True)
    gradient_blocks(
        info, spans, query, grad, log_norm, row_delta, FAR,
        (below, above), acc, (term_below, term_above),
    )


def near_backward_kernel(
    info, spans, query, log_norm, grad, row_delta, far_acc, below, own, above,
    query_grad, term_below, term_own, term_above, acc,
):
    acc[...] = far_acc[...]
    gradient_blocks(
        info, spans, query, grad, log_norm, row_delta, NEAR,
        (below, own, above), acc, (term_below, term_own, term_above),
    )
    for h, cols in COLUMNS:
        query_grad[:, cols] = (SCALE * acc[h]).T.astype(jnp.bfloat16)


def f32(*shape):
    return jax.ShapeDtypeStruct(shape, jnp.float32)


def bf16(*shape):
    return jax.ShapeDtypeStruct(shape, jnp.bfloat16)


EIGHTS = (MINE, 8, CHIP)
ROWS = (MINE, 1, CHIP)
SUMS = (MINE, HEAD, CHIP)
WINDOW = (2, CHIP, HALF)


def i32(*shape):
    return jax.ShapeDtypeStruct(shape, jnp.int32)


def memory(array):
    scalars = array.dtype == jnp.int32 and array.shape != (2, CHIP)
    return pl.BlockSpec(memory_space=pltpu.SMEM if scalars else pltpu.VMEM)


def kernel(body, name, out_shape, scratch, flops, *operands):
    specs = [memory(x) for x in operands]
    return pl.pallas_call(
        body,
        in_specs=specs,
        out_specs=[memory(x) for x in out_shape],
        out_shape=out_shape,
        scratch_shapes=[pltpu.VMEM(shape.shape, shape.dtype) for shape in scratch],
        compiler_params=pltpu.CompilerParams(vmem_limit_bytes=16 * 1024 * 1024),
        cost_estimate=pl.CostEstimate(flops=flops, bytes_accessed=0, transcendentals=0),
        name=name,
    )(*operands)


def to_chip(block, distance):
    chips = lax.axis_size("y") * lax.axis_size("z")
    route = [(i, i + distance) for i in range(chips) if 0 <= i + distance < chips]
    return lax.ppermute(block, ("y", "z"), route)


def along(axis, block, distance):
    size = lax.axis_size(axis)
    return lax.ppermute(block, axis, [(i, (i + distance) % size) for i in range(size)])


def swapped(block):
    return lax.ppermute(block, "c", SWAP)


def halves(core, matrix):
    own = lax.dynamic_slice_in_dim(matrix, core * HALF, HALF, matrix.ndim - 1)
    other = lax.dynamic_slice_in_dim(matrix, (1 - core) * HALF, HALF, matrix.ndim - 1)
    return own, other


def on_device(query, keys, values, out_grad, out_weight, lengths):
    core = lax.axis_index("c")
    x, y = lax.axis_index("x"), lax.axis_index("y")
    chip = y * lax.axis_size("z") + lax.axis_index("z")
    size_x, size_y, size_z = (lax.axis_size(a) for a in ("x", "y", "z"))
    quarter = out_grad.shape[2] // size_y

    own_kv, other_kv = (
        jnp.stack(pair) for pair in zip(halves(core, keys[0]), halves(core, values[0]))
    )
    own = jnp.concatenate([own_kv, swapped(other_kv)], axis=1)
    own, later_grad = lax.optimization_barrier((own, out_grad[0]))
    below = to_chip(own, 1)
    above = to_chip(own, -1)

    own_query, other_query = halves(core, query[0])
    chip_query = jnp.concatenate([own_query, swapped(other_query)], axis=0)
    place = jnp.stack([chip * CHIP, core]).astype(jnp.int32)
    spans, info = kernel(spans_kernel, "spans", [i32(2, CHIP), i32(4)], [], 0, place, lengths)

    def quarters(axis, place, matrix):
        def piece(distance):
            start = (place + distance) % lax.axis_size(axis) * quarter
            return lax.dynamic_slice_in_dim(matrix, start, quarter, 1)

        got = [piece(0)]
        got += [along(axis, piece(d), d) for d in range(1, lax.axis_size(axis))]
        got = jnp.stack(got)
        return got, swapped(got)

    mine, others = quarters("y", y, out_grad[0])

    rows = out_weight.shape[0]
    piece = lax.dynamic_index_in_dim(
        out_weight.reshape(rows, 2, size_x, HEAD), x, 2, keepdims=False
    )
    piece = jnp.broadcast_to(piece.transpose(1, 0, 2)[None], (size_z, 2, rows, HEAD))
    piece = lax.all_to_all(piece.reshape(2 * size_z, rows, HEAD), ("z", "c"), 0, 0)
    piece = jnp.broadcast_to(piece.reshape(1, quarter, HEAD), (size_x, quarter, HEAD))
    weight = lax.all_to_all(piece, "x", 0, 0)

    parts = kernel(
        grad_parts_kernel, "grad_parts", [bf16(CHIP, HALF)] * size_y,
        [bf16(quarter, HALF)], GRAD_PARTS, info, mine, others, weight,
    )
    parts = [parts[0]] + [along("y", parts[d], -d) for d in range(1, size_y)]
    rows_grad = jnp.stack(quarters("x", x, later_grad), axis=1).reshape(size_x * CHIP, quarter).T

    below, above, info, spans, chip_query = lax.optimization_barrier(
        (below, above, info, spans, chip_query)
    )
    far_below = to_chip(below, 1)
    far_above = to_chip(above, -1)

    near = kernel(
        near_forward_kernel, "near_forward", [f32(*EIGHTS), f32(*EIGHTS), f32(*SUMS)],
        [f32(MINE, 2 * len(NEAR), TOK, CHIP)], NEAR_FORWARD,
        info, spans, chip_query, below, own, above,
    )
    near, rows_grad = lax.optimization_barrier((near, rows_grad))
    attended, log_norm = kernel(
        far_forward_kernel, "far_forward", [bf16(CHIP, HALF), f32(*ROWS)],
        [f32(MINE, 2 * len(FAR), TOK, CHIP), f32(*EIGHTS), f32(*EIGHTS), f32(*SUMS)], FAR_FORWARD,
        info, spans, chip_query, far_below, far_above, *near,
    )
    attended_along = [attended] + [along("x", attended, d) for d in range(1, size_x)]

    grad, row_delta, far_acc, term_far_below, term_far_above = kernel(
        far_backward_kernel, "far_backward",
        [bf16(CHIP, HALF), f32(*ROWS), f32(*SUMS), bf16(*WINDOW), bf16(*WINDOW)],
        [], FAR_BACKWARD,
        info, spans, chip_query, attended, log_norm, far_below, far_above, *parts,
    )
    passed_below = to_chip(term_far_below, -1)
    passed_above = to_chip(term_far_above, 1)
    partial = nn(rows_grad, jnp.concatenate(attended_along, axis=0)).astype(jnp.bfloat16)
    partial, grad = lax.optimization_barrier((partial, grad))
    query_grad, term_below, term_own, term_above = kernel(
        near_backward_kernel, "near_backward",
        [bf16(CHIP, HALF), bf16(*WINDOW), f32(*WINDOW), bf16(*WINDOW)],
        [f32(*SUMS)], NEAR_BACKWARD,
        info, spans, chip_query, log_norm, grad, row_delta, far_acc, below, own, above,
    )
    partial = partial.reshape(size_y, -1, HALF)
    summed = 0.0
    for d in range(size_y):
        piece = lax.dynamic_index_in_dim(partial, (y + d) % size_y, 0, keepdims=False)
        summed = summed + (along("y", piece, d) if d else piece).astype(jnp.float32)
    partial = summed.astype(jnp.bfloat16)
    partial = lax.all_to_all(partial.reshape(2 * size_z, -1, HALF), ("z", "c"), 0, 0)
    partial = jnp.sum(partial.reshape(size_z, 2, -1, HALF).astype(jnp.float32), axis=0)
    weight_grad = jnp.concatenate([partial[0], partial[1]], axis=1)

    total = term_own
    for term, passed, side in ((term_below, passed_below, -1), (term_above, passed_above, 1)):
        both = (term.astype(jnp.float32) + passed.astype(jnp.float32)).astype(jnp.bfloat16)
        total = total + to_chip(both, side).astype(jnp.float32)
    grads = jnp.concatenate([query_grad[None], total.astype(jnp.bfloat16)], axis=0)
    stay = grads[:, :TOK]
    theirs = swapped(grads[:, TOK:])
    low = jnp.where(core == 0, stay, theirs)
    high = jnp.where(core == 0, theirs, stay)
    grads = jnp.concatenate([low, high], axis=2)
    return (grads[0:1], grads[1:2], grads[2:3], weight_grad)


def solution(mesh):
    fine = Mesh(mesh.devices.reshape(4, 4, 8, 2), ("x", "y", "z", "c"))
    tokens = P("x", ("y", "z", "c"), None)
    return jax.shard_map(
        on_device,
        mesh=fine,
        in_specs=(tokens, tokens, tokens, tokens, P(("y", "z", "c"), None), P("x", None)),
        out_specs=(tokens, tokens, tokens, P(("x", "y", "z", "c"), None)),
        check_vma=False,
    )
```

```python
import math

import jax
import jax.numpy as jnp
from jax import lax
from jax.experimental import pallas as pl
from jax.experimental.pallas import tpu as pltpu
from jax.sharding import Mesh, PartitionSpec as P

HEADS = 8
HEAD = 128
TOK = 128
CHIP = 2 * TOK
MINE = HEADS // 2
HALF = MINE * HEAD
NEAR = (-1, 0, 1)
FAR = (-2, 2)
SCALE = 1.0 / math.sqrt(HEAD)
LOG2E = math.log2(math.e)
GRAD_PARTS = 0
NEAR_FORWARD = 2013265920
FAR_FORWARD = 2684354560
FAR_BACKWARD = 0
NEAR_BACKWARD = 0
SWAP = [(0, 1), (1, 0)]
COLUMNS = [(h, slice(h * HEAD, (h + 1) * HEAD)) for h in range(MINE)]


def nt(a, b):
    return lax.dot_general(a, b, (((1,), (1,)), ((), ())), preferred_element_type=jnp.float32)


def nn(a, b):
    return lax.dot_general(a, b, (((1,), (0,)), ((), ())), preferred_element_type=jnp.float32)


def tn(a, b):
    return lax.dot_general(a, b, (((0,), (0,)), ((), ())), preferred_element_type=jnp.float32)


def key_blocks(info, offsets, body, other=None):
    for slot, offset in enumerate(offsets):
        for half in range(2):
            parity = info[1] if half == 0 else 1 - info[1]
            base = info[0] + offset * CHIP + parity * TOK
            rows = slice(half * TOK, (half + 1) * TOK)
            needed = jnp.logical_and(base < info[3], base + TOK > info[2])

            @pl.when(needed)
            def _(slot=slot, half=half, rows=rows, base=base):
                body(slot, 2 * slot + half, rows, base)

            if other is not None:

                @pl.when(jnp.logical_not(needed))
                def _(slot=slot, rows=rows):
                    other(slot, rows)


def block_mask(spans, base):
    position = base + lax.broadcasted_iota(jnp.int32, (TOK, CHIP), 0)
    return jnp.logical_and(position >= spans[0:1, :], position < spans[1:2, :])


def masked_scores(keys, query, taken):
    return jnp.where(taken, nt(keys, query) * (SCALE * LOG2E), -1e30)


def by_eights(block):
    return block.reshape(TOK // 8, 8, CHIP)


def over_eights(op, rows):
    return jnp.broadcast_to(op(rows, axis=0, keepdims=True), (8, CHIP))


def score_blocks(info, spans, query, offsets, windows, scores, peak):
    def body(slot, index, rows, base):
        taken = block_mask(spans, base)
        for h, cols in COLUMNS:
            block = masked_scores(windows[slot][0, rows, cols], query[:, cols], taken)
            scores[h, index] = block
            peak[h] = jnp.maximum(peak[h], jnp.max(by_eights(block), axis=0))

    key_blocks(info, offsets, body)
    for h, _ in COLUMNS:
        peak[h] = over_eights(jnp.max, peak[h])


def absorb_blocks(info, offsets, windows, scores, peak, total, acc):
    def body(slot, index, rows, base):
        for h, cols in COLUMNS:
            weights = jnp.exp2(scores[h, index] - peak[h, 0:1, :])
            total[h] += jnp.sum(by_eights(weights), axis=0)
            acc[h] += tn(windows[slot][1, rows, cols], weights.astype(jnp.bfloat16))

    key_blocks(info, offsets, body)


def spans_kernel(place, lengths, spans, info):
    first, core = place[0], place[1]
    index = lax.broadcasted_iota(jnp.int32, (1, CHIP), 1)
    swapped_index = jnp.where(index < TOK, index + TOK, index - TOK)
    positions = first + jnp.where(core == 0, index, swapped_index)
    start = jnp.zeros((1, CHIP), jnp.int32)
    end = jnp.zeros((1, CHIP), jnp.int32)
    begin, low, high = jnp.int32(0), jnp.int32(0), jnp.int32(0)
    for image in range(lengths.shape[1]):
        finish = begin + lengths[0, image]
        begun = positions >= begin
        start = jnp.where(begun, begin, start)
        end = jnp.where(begun, finish, end)
        low = jnp.where(first >= begin, begin, low)
        high = jnp.where(first + CHIP - 1 >= begin, finish, high)
        begin = finish
    spans[0:1, :] = start
    spans[1:2, :] = end
    info[0] = first
    info[1] = core
    info[2] = low
    info[3] = high


def near_forward_kernel(info, spans, query, below, own, above, peak, total, acc, scores):
    windows = (below, own, above)
    peak[...] = jnp.full(peak.shape, -1e30, jnp.float32)
    total[...] = jnp.zeros(total.shape, jnp.float32)
    acc[...] = jnp.zeros(acc.shape, jnp.float32)
    score_blocks(info, spans, query, NEAR, windows, scores, peak)
    absorb_blocks(info, NEAR, windows, scores, peak, total, acc)


def far_forward_kernel(
    info, spans, query, below, above, near_peak, near_total, near_acc,
    attended, log_norm, scores, peak, total, acc,
):
    windows = (below, above)
    peak[...] = near_peak[...]
    score_blocks(info, spans, query, FAR, windows, scores, peak)
    for h, _ in COLUMNS:
        shrink = jnp.exp2(near_peak[h] - peak[h])
        total[h] = near_total[h] * shrink
        acc[h] = near_acc[h] * shrink[0:1, :]
    absorb_blocks(info, FAR, windows, scores, peak, total, acc)
    for h, cols in COLUMNS:
        row_total = jnp.sum(total[h], axis=0, keepdims=True)
        attended[:, cols] = (acc[h] * (1.0 / row_total)).T.astype(jnp.bfloat16)
        log_norm[h] = peak[h, 0:1, :] + jnp.log(row_total) * LOG2E


def gradient_blocks(
    info, spans, query, grad, log_norm, row_delta, offsets, windows, acc, terms
):
    def body(slot, index, rows, base):
        taken = block_mask(spans, base)
        term = terms[slot]
        for h, cols in COLUMNS:
            keys = windows[slot][0, rows, cols]
            values = windows[slot][1, rows, cols]
            probs = jnp.exp2(masked_scores(keys, query[:, cols], taken) - log_norm[h])
            dprobs = nt(values, grad[:, cols])
            dscores = (probs * (dprobs - row_delta[h])).astype(jnp.bfloat16)
            acc[h] += tn(keys, dscores)
            term[0, rows, cols] = (SCALE * nn(dscores, query[:, cols])).astype(term.dtype)
            term[1, rows, cols] = nn(probs.astype(jnp.bfloat16), grad[:, cols]).astype(term.dtype)

    def other(slot, rows):
        terms[slot][:, rows, :] = jnp.zeros((2, TOK, HALF), terms[slot].dtype)

    key_blocks(info, offsets, body, other)


def grad_parts_kernel(info, own, other, weight, *rest):
    parts = rest[:-1]
    columns = rest[-1]
    for h, cols in COLUMNS:
        columns[:, cols] = weight[h]
    for slot, part in enumerate(parts):
        part[0:TOK, :] = nn(own[slot], columns[...]).astype(jnp.bfloat16)
        part[TOK:CHIP, :] = nn(other[slot], columns[...]).astype(jnp.bfloat16)


def far_backward_kernel(
    info, spans, query, attended, log_norm, below, above, *rest
):
    parts = rest[:-5]
    grad, row_delta, acc, term_below, term_above = rest[-5:]
    acc[...] = jnp.zeros(acc.shape, jnp.float32)
    for h, cols in COLUMNS:
        total = parts[0][:, cols].astype(jnp.float32)
        for part in parts[1:]:
            total = total + part[:, cols].astype(jnp.float32)
        head_grad = total.astype(jnp.bfloat16)
        grad[:, cols] = head_grad
        product = head_grad.astype(jnp.float32) * attended[:, cols].astype(jnp.float32)
        row_delta[h] = jnp.sum(product.T, axis=0, keepdims=True)
    gradient_blocks(
        info, spans, query, grad, log_norm, row_delta, FAR,
        (below, above), acc, (term_below, term_above),
    )


def near_backward_kernel(
    info, spans, query, log_norm, grad, row_delta, far_acc, below, own, above,
    query_grad, term_below, term_own, term_above, acc,
):
    acc[...] = far_acc[...]
    gradient_blocks(
        info, spans, query, grad, log_norm, row_delta, NEAR,
        (below, own, above), acc, (term_below, term_own, term_above),
    )
    for h, cols in COLUMNS:
        query_grad[:, cols] = (SCALE * acc[h]).T.astype(jnp.bfloat16)


def f32(*shape):
    return jax.ShapeDtypeStruct(shape, jnp.float32)


def bf16(*shape):
    return jax.ShapeDtypeStruct(shape, jnp.bfloat16)


EIGHTS = (MINE, 8, CHIP)
ROWS = (MINE, 1, CHIP)
SUMS = (MINE, HEAD, CHIP)
WINDOW = (2, CHIP, HALF)


def i32(*shape):
    return jax.ShapeDtypeStruct(shape, jnp.int32)


def memory(array):
    scalars = array.dtype == jnp.int32 and array.shape != (2, CHIP)
    return pl.BlockSpec(memory_space=pltpu.SMEM if scalars else pltpu.VMEM)


def kernel(body, name, out_shape, scratch, flops, *operands):
    specs = [memory(x) for x in operands]
    return pl.pallas_call(
        body,
        in_specs=specs,
        out_specs=[memory(x) for x in out_shape],
        out_shape=out_shape,
        scratch_shapes=[pltpu.VMEM(shape.shape, shape.dtype) for shape in scratch],
        compiler_params=pltpu.CompilerParams(vmem_limit_bytes=16 * 1024 * 1024),
        cost_estimate=pl.CostEstimate(flops=flops, bytes_accessed=0, transcendentals=0),
        name=name,
    )(*operands)


def to_chip(block, distance):
    chips = lax.axis_size("y") * lax.axis_size("z")
    route = [(i, i + distance) for i in range(chips) if 0 <= i + distance < chips]
    return lax.ppermute(block, ("y", "z"), route)


def along(axis, block, distance):
    size = lax.axis_size(axis)
    return lax.ppermute(block, axis, [(i, (i + distance) % size) for i in range(size)])


def swapped(block):
    return lax.ppermute(block, "c", SWAP)


def halves(core, matrix):
    own = lax.dynamic_slice_in_dim(matrix, core * HALF, HALF, matrix.ndim - 1)
    other = lax.dynamic_slice_in_dim(matrix, (1 - core) * HALF, HALF, matrix.ndim - 1)
    return own, other


def on_device(query, keys, values, out_grad, out_weight, lengths):
    core = lax.axis_index("c")
    x, y = lax.axis_index("x"), lax.axis_index("y")
    chip = y * lax.axis_size("z") + lax.axis_index("z")
    size_x, size_y, size_z = (lax.axis_size(a) for a in ("x", "y", "z"))
    quarter = out_grad.shape[2] // size_y

    own_kv, other_kv = (
        jnp.stack(pair) for pair in zip(halves(core, keys[0]), halves(core, values[0]))
    )
    own = jnp.concatenate([own_kv, swapped(other_kv)], axis=1)
    own, later_grad = lax.optimization_barrier((own, out_grad[0]))
    below = to_chip(own, 1)
    above = to_chip(own, -1)

    own_query, other_query = halves(core, query[0])
    chip_query = jnp.concatenate([own_query, swapped(other_query)], axis=0)
    place = jnp.stack([chip * CHIP, core]).astype(jnp.int32)
    spans, info = kernel(spans_kernel, "spans", [i32(2, CHIP), i32(4)], [], 0, place, lengths)

    def quarters(axis, place, matrix):
        def piece(distance):
            start = (place + distance) % lax.axis_size(axis) * quarter
            return lax.dynamic_slice_in_dim(matrix, start, quarter, 1)

        got = [piece(0)]
        got += [along(axis, piece(d), d) for d in range(1, lax.axis_size(axis))]
        got = jnp.stack(got)
        return got, swapped(got)

    mine, others = quarters("y", y, out_grad[0])

    rows = out_weight.shape[0]
    piece = lax.dynamic_index_in_dim(
        out_weight.reshape(rows, 2, size_x, HEAD), x, 2, keepdims=False
    )
    piece = jnp.broadcast_to(piece.transpose(1, 0, 2)[None], (size_z, 2, rows, HEAD))
    piece = lax.all_to_all(piece.reshape(2 * size_z, rows, HEAD), ("z", "c"), 0, 0)
    piece = jnp.broadcast_to(piece.reshape(1, quarter, HEAD), (size_x, quarter, HEAD))
    weight = lax.all_to_all(piece, "x", 0, 0)

    parts = kernel(
        grad_parts_kernel, "grad_parts", [bf16(CHIP, HALF)] * size_y,
        [bf16(quarter, HALF)], GRAD_PARTS, info, mine, others, weight,
    )
    parts = [parts[0]] + [along("y", parts[d], -d) for d in range(1, size_y)]
    rows_grad = jnp.stack(quarters("x", x, later_grad), axis=1).reshape(size_x * CHIP, quarter).T

    below, above, info, spans, chip_query = lax.optimization_barrier(
        (below, above, info, spans, chip_query)
    )
    far_below = to_chip(below, 1)
    far_above = to_chip(above, -1)

    near = kernel(
        near_forward_kernel, "near_forward", [f32(*EIGHTS), f32(*EIGHTS), f32(*SUMS)],
        [f32(MINE, 2 * len(NEAR), TOK, CHIP)], NEAR_FORWARD,
        info, spans, chip_query, below, own, above,
    )
    near, rows_grad = lax.optimization_barrier((near, rows_grad))
    attended, log_norm = kernel(
        far_forward_kernel, "far_forward", [bf16(CHIP, HALF), f32(*ROWS)],
        [f32(MINE, 2 * len(FAR), TOK, CHIP), f32(*EIGHTS), f32(*EIGHTS), f32(*SUMS)], FAR_FORWARD,
        info, spans, chip_query, far_below, far_above, *near,
    )
    attended_along = [attended] + [along("x", attended, d) for d in range(1, size_x)]

    grad, row_delta, far_acc, term_far_below, term_far_above = kernel(
        far_backward_kernel, "far_backward",
        [bf16(CHIP, HALF), f32(*ROWS), f32(*SUMS), bf16(*WINDOW), bf16(*WINDOW)],
        [], FAR_BACKWARD,
        info, spans, chip_query, attended, log_norm, far_below, far_above, *parts,
    )
    passed_below = to_chip(term_far_below, -1)
    passed_above = to_chip(term_far_above, 1)
    partial = nn(rows_grad, jnp.concatenate(attended_along, axis=0)).astype(jnp.bfloat16)
    partial, grad = lax.optimization_barrier((partial, grad))
    query_grad, term_below, term_own, term_above = kernel(
        near_backward_kernel, "near_backward",
        [bf16(CHIP, HALF), bf16(*WINDOW), f32(*WINDOW), bf16(*WINDOW)],
        [f32(*SUMS)], NEAR_BACKWARD,
        info, spans, chip_query, log_norm, grad, row_delta, far_acc, below, own, above,
    )
    both = [
        (term.astype(jnp.float32) + passed.astype(jnp.float32)).astype(jnp.bfloat16)
        for term, passed in ((term_below, passed_below), (term_above, passed_above))
    ]
    partial, both[0] = lax.optimization_barrier((partial, both[0]))
    returned = [to_chip(both[0], -1), to_chip(both[1], 1)]
    partial = lax.all_to_all(
        partial.reshape(2 * size_y * size_z, -1, HALF), ("y", "z", "c"), 0, 0
    )
    partial = partial.reshape(size_y * size_z, 2, -1, HALF)
    partial = jnp.sum(partial.astype(jnp.float32), axis=0)
    weight_grad = jnp.concatenate([partial[0], partial[1]], axis=1)

    total = term_own
    for part in returned:
        total = total + part.astype(jnp.float32)
    grads = jnp.concatenate([query_grad[None], total.astype(jnp.bfloat16)], axis=0)
    stay = grads[:, :TOK]
    theirs = swapped(grads[:, TOK:])
    low = jnp.where(core == 0, stay, theirs)
    high = jnp.where(core == 0, theirs, stay)
    grads = jnp.concatenate([low, high], axis=2)
    return (grads[0:1], grads[1:2], grads[2:3], weight_grad)


def solution(mesh):
    fine = Mesh(mesh.devices.reshape(4, 4, 8, 2), ("x", "y", "z", "c"))
    tokens = P("x", ("y", "z", "c"), None)
    return jax.shard_map(
        on_device,
        mesh=fine,
        in_specs=(tokens, tokens, tokens, tokens, P(("y", "z", "c"), None), P("x", None)),
        out_specs=(tokens, tokens, tokens, P(("x", "y", "z", "c"), None)),
        check_vma=False,
    )
```
